512 devices in a mesh: date: 32 (over z_hi, y, x), col: 16 (over z_lo, core).
Axes of the slice: x: 4, y: 4, z: 16 (z_hi: 2, z_lo: 8; z = z_hi * 8 + z_lo), core: 2. Of those that a mesh axis runs over, the one named last changes fastest.
Arguments:
- slc: float32 [192, 2, 20, 16384], P('date', None, None, 'col'), may hold values from -130 to 130, as said below
- first_row: int32 [192], P('date'), may hold values from 0 to 4
- stop_row: int32 [192], P('date'), may hold values from 16 to 20
- pair_used: int32 [192, 4], P('date'), may hold values 0 or 1
Outputs:
- coherence: float32 [192, 4, 3, 4, 16384], P('date', None, None, None, 'col')
The draws below stay inside these ranges and needn't reach their ends.
Inputs may be any that keep to these rules, and one draw needn't show every extreme that they name: `slc`: finite values.
All inputs are finite; a program needn't handle non-finite values. No bound on the sum of `pair_used` on one device may be relied on, other than what follows from the above.
Results may differ from the reference program's by a relative error of at most 0.0001.
Values sent between devices are 32-bit elements; how exact they have to be, the bound alone decides.
No kernel may reach another device: no remote copies, remote signals or barrier semaphores. Data moves between devices by JAX's collectives and lax.ppermute only.
A program may use at most 64 MiB of HBM per device.

```python
import math
import jax
import jax.numpy as jnp

LAG = 4
AZ_LOOKS = 5
RG_LOOKS = 20
ROWS = 20
DATES = 192
COLS = 16384


def draw_slc(key, part):
    key = jax.random.fold_in(key, 11)
    keys = jax.random.split(key, 4)
    common = jnp.clip(jax.random.normal(keys[0], (2, ROWS, COLS), jnp.float32), -4.0, 4.0)
    amplitude = jnp.exp(jax.random.uniform(keys[1], (ROWS, COLS), jnp.float32, 0.0, math.log(10.0)))
    noise = jnp.clip(jax.random.normal(keys[2], (DATES, 2, ROWS, COLS), jnp.float32), -4.0, 4.0)
    phase = jax.random.uniform(keys[3], (DATES, ROWS, COLS), jnp.float32, -1.2, 1.2)
    cosine = jnp.cos(phase)
    sine = jnp.sin(phase)
    real_part = common[0][None] * cosine - common[1][None] * sine
    imag_part = common[0][None] * sine + common[1][None] * cosine
    signal = jnp.stack([real_part, imag_part], axis=1)
    return amplitude[None, None] * (signal + 0.5 * noise)


def plant(drawn, stream_key, low, top_value):
    spot = [jax.random.randint(jax.random.fold_in(stream_key, axis), (), 0, length) for axis, length in enumerate(drawn.shape)]
    widest = drawn.shape.index(max(drawn.shape))
    next_to = spot[:widest] + [(spot[widest] + 1) % drawn.shape[widest]] + spot[widest + 1:]
    return drawn.at[tuple(spot)].set(low).at[tuple(next_to)].set(top_value)


def setup_inputs(seed: int = 0) -> dict:
    key_list = jax.random.split(jax.random.key(seed), 5)
    return {
        "slc": draw_slc(jax.random.fold_in(key_list[4], 71), 0),
        "first_row": plant(jax.random.randint(key_list[1], (DATES,), 0, ROWS // 4), jax.random.fold_in(key_list[1], 1), 0, (ROWS // 4) - 1).astype(jnp.int32),
        "stop_row": plant(jax.random.randint(key_list[2], (DATES,), 3 * ROWS // 4 + 1, ROWS + 1), jax.random.fold_in(key_list[2], 1), 3 * ROWS // 4 + 1, ROWS).astype(jnp.int32),
        "pair_used": plant((jax.random.randint(key_list[3], (DATES, LAG), 0, 4) < 3).astype(jnp.int32), jax.random.fold_in(key_list[3], 1), 0, 1),
    }


def box_sum(values):
    array_shape = values.shape
    folded = values.reshape(array_shape[:-2] + (array_shape[-2] // AZ_LOOKS, AZ_LOOKS, array_shape[-1])).sum(axis=-2)
    margin = RG_LOOKS // 2
    padded = jnp.pad(folded, [(0, 0)] * (folded.ndim - 1) + [(margin, margin)])
    col_count = folded.shape[-1]
    running = padded[..., 0:col_count]
    for offset in range(1, RG_LOOKS):
        running = running + padded[..., offset:offset + col_count]
    return running

def coherence_of(cross_real, cross_imag, power_first, power_second, used):
    scale_down = jnp.sqrt(jnp.maximum(power_first * power_second, 1.0))
    gamma_real = cross_real * used / scale_down
    gamma_imag = cross_imag * used / scale_down
    magnitude = jnp.sqrt(gamma_real * gamma_real + gamma_imag * gamma_imag)
    return jnp.stack([gamma_real, gamma_imag, magnitude], axis=-3)

def reference(slc, first_row, stop_row, pair_used):
    row_index = jnp.arange(ROWS, dtype=jnp.int32)
    valid = ((row_index[None, :] >= first_row[:, None]) & (row_index[None, :] < stop_row[:, None])).astype(jnp.float32)
    masked = slc * valid[:, None, :, None]
    extended = jnp.concatenate([masked, jnp.zeros((LAG,) + masked.shape[1:], jnp.float32)], axis=0)
    powers = box_sum(extended[:, 0] * extended[:, 0] + extended[:, 1] * extended[:, 1])
    results = []
    for offset in range(LAG):
        partner = extended[offset + 1:offset + 1 + DATES]
        cross_real = masked[:, 0] * partner[:, 0] + masked[:, 1] * partner[:, 1]
        cross_imag = masked[:, 1] * partner[:, 0] - masked[:, 0] * partner[:, 1]
        used = pair_used[:, offset].astype(jnp.float32)[:, None, None]
        results.append(coherence_of(box_sum(cross_real), box_sum(cross_imag), powers[:DATES], powers[offset + 1:offset + 1 + DATES], used))
    return jnp.stack(results, axis=1)
```

```python
import functools

import jax
import jax.numpy as jnp
from jax import lax
from jax.experimental import pallas as pl
from jax.experimental.pallas import tpu as pltpu
from jax.sharding import PartitionSpec as P

AZ = 5
LAG = 4
DATES = 6
LOOKS = 4
COLS = 1024
LANES = 128
CHUNKS = COLS // LANES
WIDE = COLS + LANES
AXES = ("date", "col")

PIECES = (7, 7, 6)
COLUMN_SETS = (
    ((0, 0), (3, 0), (0, 3)),
    ((3, 3), (1, 0), (0, 1)),
    ((2, 3), (3, 2), (1, 3)),
    ((3, 1), (2, 0), (0, 2)),
)
SOURCE_XY = (0, 0)
TARGET_XY = (3, 3)

INNER_PAIRS = [(i, k) for i in range(DATES) for k in range(LAG) if i + k + 1 < DATES]
OUTER_PAIRS = [(i, k) for i in range(DATES) for k in range(LAG) if i + k + 1 >= DATES]

VMEM = pl.BlockSpec(memory_space=pltpu.VMEM)
SMEM = pl.BlockSpec(memory_space=pltpu.SMEM)
ANY = pl.BlockSpec(memory_space=pl.ANY)


def lane_roll(x, by):
    return pltpu.roll(x, by % x.shape[-1], axis=x.ndim - 1)


def half_swap(x):
    return pltpu.roll(x, LOOKS, axis=0)


def window(x):
    s2 = x + lane_roll(x, -1)
    s4 = s2 + lane_roll(s2, 2)
    s8 = s4 + lane_roll(s4, -4)
    s16 = s8 + lane_roll(s8, 8)
    return (s16 + lane_roll(s4, -8))[:, :COLS]


def prepare(slc, first, stop, *refs):
    own_low, own_high, edge_low, edge_high = refs[:4]
    pieces = refs[4 : 4 + len(PIECES)]
    buf, sems = refs[4 + len(PIECES) :]

    def copy(j):
        return pltpu.make_async_copy(
            slc.at[:, :, :, pl.ds(j * LANES, LANES)], buf.at[j], sems.at[j]
        )

    for j in range(CHUNKS):
        copy(j).start()
    row = AZ * lax.broadcasted_iota(jnp.int32, (LOOKS, LANES), 0)
    starts = [sum(PIECES[:n]) for n in range(len(PIECES))]
    for j in range(CHUNKS):
        copy(j).wait()
        lanes = slice(j * LANES, (j + 1) * LANES)
        for d in range(DATES):
            for q in range(AZ):
                keep = (row + q >= first[d]) & (row + q < stop[d])
                tile = []
                for part in range(2):
                    value = buf[j, d, part, pl.ds(q, LOOKS, stride=AZ), :]
                    tile.append(jnp.where(keep, value, 0.0))
                tile = jnp.concatenate(tile, axis=0)
                if d < LAG:
                    own_low[d, q, :, lanes] = tile
                    unit = d * AZ + q
                    for start, size, piece in zip(starts, PIECES, pieces):
                        if start <= unit < start + size:
                            piece[unit - start, :, lanes] = tile
                else:
                    own_high[d - LAG, q, :, lanes] = tile
                if j == 0:
                    edge_low[d, q] = tile
                if j == CHUNKS - 1:
                    edge_high[d, q] = tile


def products(a, b, b_swapped):
    straight = a[0] * b[0]
    crossed = a[0] * b_swapped[0]
    for q in range(1, AZ):
        straight = straight + a[q] * b[q]
        crossed = crossed + a[q] * b_swapped[q]
    upper = lax.broadcasted_iota(jnp.int32, straight.shape, 0) < LOOKS
    return jnp.where(
        upper, straight + half_swap(straight), crossed - half_swap(crossed)
    )


def power_of(a):
    total = a[0] * a[0]
    for q in range(1, AZ):
        total = total + a[q] * a[q]
    return total + half_swap(total)


def write_pair(store, cross, power_first, power_second, used):
    gamma = window(cross) * (
        used * lax.rsqrt(jnp.maximum(power_first * power_second, 1.0))
    )
    square = gamma * gamma
    magnitude = jnp.sqrt(square + half_swap(square))
    store(0, gamma[:LOOKS])
    store(1, gamma[LOOKS:])
    store(2, magnitude[:LOOKS])


def inner(own_low, own_high, right, left, used, out, power, packed, sums, powers):
    lane = lax.broadcasted_iota(jnp.int32, (8, LANES), 1)

    def chunk(tiles, lanes):
        swapped = [None] + [[half_swap(t) for t in tiles[d]] for d in range(1, DATES)]
        for d in range(DATES):
            powers[d, :, lanes] = power_of(tiles[d])
        for n, (i, k) in enumerate(INNER_PAIRS):
            j = i + k + 1
            sums[n, :, lanes] = products(tiles[i], tiles[j], swapped[j])

    halo = [
        [jnp.where(lane < LANES // 2, right[d, q], left[d, q]) for q in range(AZ)]
        for d in range(DATES)
    ]
    for q in range(AZ):
        merged = halo[0][q]
        for d in range(1, LAG):
            here = (lane >= 32 * d - 16) & (lane < 32 * d + 16)
            merged = jnp.where(here, lane_roll(halo[d][q], 32 * d), merged)
        packed[q] = merged
    chunk(halo, pl.ds(COLS, LANES))

    @pl.loop(0, CHUNKS)
    def _(c):
        lanes = pl.ds(pl.multiple_of(c * LANES, LANES), LANES)
        chunk(
            [[own_low[d, q, :, lanes] for q in range(AZ)] for d in range(LAG)]
            + [[own_high[d, q, :, lanes] for q in range(AZ)] for d in range(DATES - LAG)],
            lanes,
        )

    for d in range(DATES):
        power[d] = window(powers[d])
    for n, (i, k) in enumerate(INNER_PAIRS):

        def store(m, value, i=i, k=k):
            out[i, k, m] = value

        write_pair(
            store,
            sums[n],
            power[i],
            power[i + k + 1],
            used[i, k].astype(jnp.float32),
        )


def outer(own_low, own_high, right, left, power, used, received, packed, *refs):
    count = len(PIECES)
    pieces = refs[:count]
    out, sums, powers, staged, sems = refs[count + 1 :]
    lane = lax.broadcasted_iota(jnp.int32, (8, LANES), 1)
    starts = [sum(PIECES[:n]) for n in range(count)]
    firsts = sorted({i for i, _ in OUTER_PAIRS})

    def chunk(mine, theirs, lanes):
        swapped = [[half_swap(t) for t in tiles] for tiles in theirs]
        for d in range(LAG):
            powers[d, :, lanes] = power_of(theirs[d])
        for n, (i, k) in enumerate(OUTER_PAIRS):
            j = i + k + 1 - DATES
            sums[n, :, lanes] = products(mine[i], theirs[j], swapped[j])

    chunk(
        {
            d: [jnp.where(lane < LANES // 2, right[d, q], left[d, q]) for q in range(AZ)]
            for d in firsts
        },
        [[lane_roll(packed[q], -32 * d) for q in range(AZ)] for d in range(LAG)],
        pl.ds(COLS, LANES),
    )

    @pl.loop(0, CHUNKS)
    def _(c):
        lanes = pl.ds(pl.multiple_of(c * LANES, LANES), LANES)
        mine = {}
        for d in firsts:
            ref, at = (own_low, d) if d < LAG else (own_high, d - LAG)
            mine[d] = [ref[at, q, :, lanes] for q in range(AZ)]
        theirs = []
        for d in range(LAG):
            tiles = []
            for q in range(AZ):
                unit = d * AZ + q
                tile = received[d, q, :, lanes]
                for start, size, piece in zip(starts, PIECES, pieces):
                    if start <= unit < start + size:
                        tile = tile + piece[unit - start, :, lanes]
                tiles.append(tile)
            theirs.append(tiles)
        chunk(mine, theirs, lanes)

    their_power = [window(powers[d]) for d in range(LAG)]
    copies = []
    for n, (i, k) in enumerate(OUTER_PAIRS):

        def store(m, value, n=n):
            staged[n, m] = value

        write_pair(
            store,
            sums[n],
            power[i],
            their_power[i + k + 1 - DATES],
            used[i, k].astype(jnp.float32),
        )
        copies.append(pltpu.make_async_copy(staged.at[n], out.at[i, k], sems.at[n]))
        copies[-1].start()
    for copy in copies:
        copy.wait()


def far_permutes():
    def flat(x, y, z, core):
        return ((z // 8) * 16 + y * 4 + x) * 16 + (z % 8) * 2 + core

    scatter = [[] for _ in PIECES]
    gather = [[] for _ in PIECES]
    for z in range(8):
        for core in range(2):
            for n, (x, y) in enumerate(COLUMN_SETS[z // 2][: len(PIECES)]):
                relay = flat(x, y, 8 + z, core)
                scatter[n].append((flat(*SOURCE_XY, 8 + z, core), relay))
                gather[n].append((relay, flat(*TARGET_XY, z, core)))
    return scatter, gather


def f32(*shape):
    return jax.ShapeDtypeStruct(shape, jnp.float32)


def on_device(slc, first_row, stop_row, pair_used):
    rest = DATES - LAG
    own_low, own_high, edge_low, edge_high, *pieces = pl.pallas_call(
        prepare,
        out_shape=[
            f32(LAG, AZ, 8, COLS),
            f32(rest, AZ, 8, COLS),
            f32(DATES, AZ, 8, LANES),
            f32(DATES, AZ, 8, LANES),
        ]
        + [f32(size, 8, COLS) for size in PIECES],
        in_specs=[ANY, SMEM, SMEM],
        out_specs=[VMEM] * (4 + len(PIECES)),
        scratch_shapes=[
            pltpu.VMEM((CHUNKS, DATES, 2, AZ * LOOKS, LANES), jnp.float32),
            pltpu.SemaphoreType.DMA((CHUNKS,)),
        ],
        name="prepare",
    )(slc, first_row, stop_row)

    def permute(value, pairs):
        return lax.ppermute(value, AXES, pairs)

    near = [
        (d * 16 + c, (d - 1) * 16 + c) for d in range(1, 32) if d != 16 for c in range(16)
    ]
    far = [(16 * 16 + c, 15 * 16 + c) for c in range(16)]
    to_right = [(d * 16 + c, d * 16 + c + 1) for d in range(32) for c in range(15)]
    to_left = [(b, a) for a, b in to_right]
    scatter, gather = far_permutes()
    scattered = [permute(piece, pairs) for piece, pairs in zip(pieces, scatter)]
    received = permute(own_low, near)
    left = permute(edge_high, to_right)
    right = permute(edge_low, to_left)
    gathered = [permute(piece, pairs) for piece, pairs in zip(scattered, gather)]

    out_shape = f32(DATES, LAG, 3, LOOKS, COLS)
    out, power, packed = pl.pallas_call(
        inner,
        out_shape=[out_shape, f32(DATES, 8, COLS), f32(AZ, 8, LANES)],
        in_specs=[VMEM] * 4 + [SMEM],
        out_specs=[VMEM] * 3,
        scratch_shapes=[
            pltpu.VMEM((len(INNER_PAIRS), 8, WIDE), jnp.float32),
            pltpu.VMEM((DATES, 8, WIDE), jnp.float32),
        ],
        name="inner",
    )(own_low, own_high, right, left, pair_used)
    their_packed = permute(packed, near + far)
    count = len(PIECES)
    return pl.pallas_call(
        outer,
        out_shape=out_shape,
        in_specs=[VMEM] * 5 + [SMEM] + [VMEM] * (2 + count) + [ANY],
        out_specs=ANY,
        input_output_aliases={8 + count: 0},
        scratch_shapes=[
            pltpu.VMEM((len(OUTER_PAIRS), 8, WIDE), jnp.float32),
            pltpu.VMEM((LAG, 8, WIDE), jnp.float32),
            pltpu.VMEM((len(OUTER_PAIRS), 3, LOOKS, COLS), jnp.float32),
            pltpu.SemaphoreType.DMA((len(OUTER_PAIRS),)),
        ],
        name="outer",
    )(own_low, own_high, right, left, power, pair_used, received, their_packed, *gathered, out)


def solution(mesh):
    return jax.shard_map(
        on_device,
        mesh=mesh,
        in_specs=(P("date", None, None, "col"), P("date"), P("date"), P("date", None)),
        out_specs=P("date", None, None, None, "col"),
        check_vma=False,
    )
```

```python
import functools

import jax
import jax.numpy as jnp
from jax import lax
from jax.experimental import pallas as pl
from jax.experimental.pallas import tpu as pltpu
from jax.sharding import PartitionSpec as P

AZ = 5
LAG = 4
DATES = 6
LOOKS = 4
COLS = 1024
LANES = 128
CHUNKS = COLS // LANES
WIDE = COLS + LANES
AXES = ("date", "col")

SLOT = LANES // LAG

PIECES = (7, 7, 6)
COLUMN_SETS = (
    ((0, 0), (3, 0), (0, 3)),
    ((3, 3), (1, 0), (0, 1)),
    ((2, 3), (3, 2), (1, 3)),
    ((3, 1), (2, 0), (0, 2)),
)
SOURCE_XY = (0, 0)
TARGET_XY = (3, 3)

INNER_PAIRS = [(i, k) for i in range(DATES) for k in range(LAG) if i + k + 1 < DATES]
OUTER_PAIRS = [(i, k) for i in range(DATES) for k in range(LAG) if i + k + 1 >= DATES]

VMEM = pl.BlockSpec(memory_space=pltpu.VMEM)
SMEM = pl.BlockSpec(memory_space=pltpu.SMEM)
ANY = pl.BlockSpec(memory_space=pl.ANY)


def lane_roll(x, by):
    return pltpu.roll(x, by % x.shape[-1], axis=x.ndim - 1)


def half_swap(x):
    return pltpu.roll(x, LOOKS, axis=0)


def window(x):
    s2 = x + lane_roll(x, -1)
    s4 = s2 + lane_roll(s2, 2)
    s8 = s4 + lane_roll(s4, -4)
    s16 = s8 + lane_roll(s8, 8)
    return (s16 + lane_roll(s4, -8))[:, :COLS]


def prepare(slc, first, stop, *refs):
    own_low, own_high, edge_low, edge_high = refs[:4]
    pieces = refs[4 : 4 + len(PIECES)]
    buf, sems = refs[4 + len(PIECES) :]
    rows = 2 * CHUNKS
    per_date = AZ * LOOKS * rows

    def copy(d):
        here = pl.ds(d * per_date, per_date)
        return pltpu.make_async_copy(slc.at[here], buf.at[here], sems.at[d])

    for d in range(DATES):
        copy(d).start()
    look_row = AZ * (lax.broadcasted_iota(jnp.int32, (8, LANES), 0) % LOOKS)
    lane = lax.broadcasted_iota(jnp.int32, (8, LANES), 1)
    starts = [sum(PIECES[:n]) for n in range(len(PIECES))]
    for d in range(DATES):
        copy(d).wait()
        for q in range(AZ):
            keep = (look_row + q >= first[d]) & (look_row + q < stop[d])
            for j in range(CHUNKS):
                lanes = slice(j * LANES, (j + 1) * LANES)
                base = d * per_date + q * rows + 2 * j
                tile = jnp.concatenate(
                    [
                        buf[pl.ds(base + part, LOOKS, stride=AZ * rows), :]
                        for part in range(2)
                    ],
                    axis=0,
                )
                tile = jnp.where(keep, tile, 0.0)
                if d < LAG:
                    own_low[d, q, :, lanes] = tile
                    unit = d * AZ + q
                    for start, size, piece in zip(starts, PIECES, pieces):
                        if start <= unit < start + size:
                            piece[unit - start, :, lanes] = tile
                else:
                    own_high[d - LAG, q, :, lanes] = tile
                for edge, at, begin in (
                    (edge_low, 0, 0),
                    (edge_high, CHUNKS - 1, -SLOT // 2),
                ):
                    if j == at:
                        slot = d % LAG
                        here = (lane - SLOT * slot - begin) % LANES < SLOT // 2
                        moved = lane_roll(tile, SLOT * slot)
                        rest = 0.0 if slot == 0 else edge[d // LAG, q]
                        edge[d // LAG, q] = jnp.where(here, moved, rest)


def products(a, b, b_swapped):
    straight = a[0] * b[0]
    crossed = a[0] * b_swapped[0]
    for q in range(1, AZ):
        straight = straight + a[q] * b[q]
        crossed = crossed + a[q] * b_swapped[q]
    upper = lax.broadcasted_iota(jnp.int32, straight.shape, 0) < LOOKS
    return jnp.where(
        upper, straight + half_swap(straight), crossed - half_swap(crossed)
    )


def power_of(a):
    total = a[0] * a[0]
    for q in range(1, AZ):
        total = total + a[q] * a[q]
    return total + half_swap(total)


def write_pair(store, cross, power_first, power_second, used):
    gamma = window(cross) * (
        used * lax.rsqrt(jnp.maximum(power_first * power_second, 1.0))
    )
    square = gamma * gamma
    magnitude = jnp.sqrt(square + half_swap(square))
    store(0, gamma[:LOOKS])
    store(1, gamma[LOOKS:])
    store(2, magnitude[:LOOKS])


def halo_of(edges, d):
    return [lane_roll(edges[d // LAG, q], -SLOT * (d % LAG)) for q in range(AZ)]


def inner(own_low, own_high, edges, used, out, power, sums, powers):
    def chunk(tiles, lanes):
        swapped = [None] + [[half_swap(t) for t in tiles[d]] for d in range(1, DATES)]
        for d in range(DATES):
            powers[d, :, lanes] = power_of(tiles[d])
        for n, (i, k) in enumerate(INNER_PAIRS):
            j = i + k + 1
            sums[n, :, lanes] = products(tiles[i], tiles[j], swapped[j])

    halo = [halo_of(edges, d) for d in range(DATES)]
    chunk(halo, pl.ds(COLS, LANES))

    @pl.loop(0, CHUNKS)
    def _(c):
        lanes = pl.ds(pl.multiple_of(c * LANES, LANES), LANES)
        chunk(
            [[own_low[d, q, :, lanes] for q in range(AZ)] for d in range(LAG)]
            + [[own_high[d, q, :, lanes] for q in range(AZ)] for d in range(DATES - LAG)],
            lanes,
        )

    for d in range(DATES):
        power[d] = window(powers[d])
    for n, (i, k) in enumerate(INNER_PAIRS):

        def store(m, value, i=i, k=k):
            out[i, k, m] = value

        write_pair(
            store,
            sums[n],
            power[i],
            power[i + k + 1],
            used[i, k].astype(jnp.float32),
        )


def outer(own_low, own_high, edges, power, used, received, their_edges, *refs):
    count = len(PIECES)
    pieces = refs[:count]
    out, sums, powers, staged, sems = refs[count + 1 :]
    starts = [sum(PIECES[:n]) for n in range(count)]
    firsts = sorted({i for i, _ in OUTER_PAIRS})

    def chunk(mine, theirs, lanes):
        swapped = [[half_swap(t) for t in tiles] for tiles in theirs]
        for d in range(LAG):
            powers[d, :, lanes] = power_of(theirs[d])
        for n, (i, k) in enumerate(OUTER_PAIRS):
            j = i + k + 1 - DATES
            sums[n, :, lanes] = products(mine[i], theirs[j], swapped[j])

    chunk(
        {d: halo_of(edges, d) for d in firsts},
        [halo_of(their_edges, d) for d in range(LAG)],
        pl.ds(COLS, LANES),
    )

    @pl.loop(0, CHUNKS)
    def _(c):
        lanes = pl.ds(pl.multiple_of(c * LANES, LANES), LANES)
        mine = {}
        for d in firsts:
            ref, at = (own_low, d) if d < LAG else (own_high, d - LAG)
            mine[d] = [ref[at, q, :, lanes] for q in range(AZ)]
        theirs = []
        for d in range(LAG):
            tiles = []
            for q in range(AZ):
                unit = d * AZ + q
                tile = received[d, q, :, lanes]
                for start, size, piece in zip(starts, PIECES, pieces):
                    if start <= unit < start + size:
                        tile = tile + piece[unit - start, :, lanes]
                tiles.append(tile)
            theirs.append(tiles)
        chunk(mine, theirs, lanes)

    their_power = [window(powers[d]) for d in range(LAG)]
    copies = []
    for n, (i, k) in enumerate(OUTER_PAIRS):

        def store(m, value, n=n):
            staged[n, m] = value

        write_pair(
            store,
            sums[n],
            power[i],
            their_power[i + k + 1 - DATES],
            used[i, k].astype(jnp.float32),
        )
        copies.append(pltpu.make_async_copy(staged.at[n], out.at[i, k], sems.at[n]))
        copies[-1].start()
    for copy in copies:
        copy.wait()


def far_permutes():
    def flat(x, y, z, core):
        return ((z // 8) * 16 + y * 4 + x) * 16 + (z % 8) * 2 + core

    scatter = [[] for _ in PIECES]
    gather = [[] for _ in PIECES]
    for z in range(8):
        for core in range(2):
            for n, (x, y) in enumerate(COLUMN_SETS[z // 2][: len(PIECES)]):
                relay = flat(x, y, 8 + z, core)
                scatter[n].append((flat(*SOURCE_XY, 8 + z, core), relay))
                gather[n].append((relay, flat(*TARGET_XY, z, core)))
    return scatter, gather


def f32(*shape):
    return jax.ShapeDtypeStruct(shape, jnp.float32)


def on_device(slc, first_row, stop_row, pair_used):
    rest = DATES - LAG
    flat = slc.reshape(DATES, 2, AZ * LOOKS, CHUNKS, LANES).transpose(0, 2, 3, 1, 4)
    flat = flat.reshape(DATES * AZ * LOOKS * CHUNKS * 2, LANES)
    own_low, own_high, edge_low, edge_high, *pieces = pl.pallas_call(
        prepare,
        out_shape=[
            f32(LAG, AZ, 8, COLS),
            f32(rest, AZ, 8, COLS),
            f32(2, AZ, 8, LANES),
            f32(2, AZ, 8, LANES),
        ]
        + [f32(size, 8, COLS) for size in PIECES],
        in_specs=[ANY, SMEM, SMEM],
        out_specs=[VMEM] * (4 + len(PIECES)),
        scratch_shapes=[
            pltpu.VMEM(flat.shape, jnp.float32),
            pltpu.SemaphoreType.DMA((DATES,)),
        ],
        name="prepare",
    )(flat, first_row, stop_row)

    def permute(value, pairs):
        return lax.ppermute(value, AXES, pairs)

    near = [
        (d * 16 + c, (d - 1) * 16 + c) for d in range(1, 32) if d != 16 for c in range(16)
    ]
    far = [(16 * 16 + c, 15 * 16 + c) for c in range(16)]
    to_right = [(d * 16 + c, d * 16 + c + 1) for d in range(32) for c in range(15)]
    to_left = [(b, a) for a, b in to_right]
    scatter, gather = far_permutes()
    scattered = [permute(piece, pairs) for piece, pairs in zip(pieces, scatter)]
    received = permute(own_low, near)
    left = permute(edge_high, to_right)
    right = permute(edge_low, to_left)
    edges = right + left
    their_edges = permute(edges[:1], near + far)
    gathered = [permute(piece, pairs) for piece, pairs in zip(scattered, gather)]

    out_shape = f32(DATES, LAG, 3, LOOKS, COLS)
    out, power = pl.pallas_call(
        inner,
        out_shape=[out_shape, f32(DATES, 8, COLS)],
        in_specs=[VMEM] * 3 + [SMEM],
        out_specs=[VMEM] * 2,
        scratch_shapes=[
            pltpu.VMEM((len(INNER_PAIRS), 8, WIDE), jnp.float32),
            pltpu.VMEM((DATES, 8, WIDE), jnp.float32),
        ],
        name="inner",
    )(own_low, own_high, edges, pair_used)
    count = len(PIECES)
    return pl.pallas_call(
        outer,
        out_shape=out_shape,
        in_specs=[VMEM] * 4 + [SMEM] + [VMEM] * (2 + count) + [ANY],
        out_specs=ANY,
        input_output_aliases={7 + count: 0},
        scratch_shapes=[
            pltpu.VMEM((len(OUTER_PAIRS), 8, WIDE), jnp.float32),
            pltpu.VMEM((LAG, 8, WIDE), jnp.float32),
            pltpu.VMEM((len(OUTER_PAIRS), 3, LOOKS, COLS), jnp.float32),
            pltpu.SemaphoreType.DMA((len(OUTER_PAIRS),)),
        ],
        name="outer",
    )(
        own_low,
        own_high,
        edges,
        power,
        pair_used,
        received,
        their_edges,
        *gathered,
        out,
    )


def solution(mesh):
    return jax.shard_map(
        on_device,
        mesh=mesh,
        in_specs=(P("date", None, None, "col"), P("date"), P("date"), P("date", None)),
        out_specs=P("date", None, None, None, "col"),
        check_vma=False,
    )
```

```python
import jax
import jax.numpy as jnp
from jax import lax
from jax.experimental import pallas as pl
from jax.experimental.pallas import tpu as pltpu
from jax.sharding import PartitionSpec as P

AZ = 5
LAG = 4
DATES = 6
LOOKS = 4
COLS = 1024
MARGIN = 10
LANES = 128
CHUNKS = COLS // LANES
GROUP = 2 * LANES
ROW = 2 * CHUNKS
PER_DATE = AZ * LOOKS * ROW
WIDE = COLS + 2 * LANES
AXES = ("date", "col")

SLOT = LANES // LAG

PIECES = (10, 10)
COUNT = len(PIECES)
STARTS = [sum(PIECES[:n]) for n in range(COUNT)]
COLUMN_SETS = (
    (((0, 0), (3, 0)), ((0, 3), (3, 3))),
    (((1, 0), (0, 1)), ((2, 3), (3, 2))),
    (((2, 0), (0, 2)), ((1, 3), (3, 1))),
    (((1, 1), (2, 2)), ((2, 1), (1, 2))),
)
SOURCE_XY = (0, 0)
TARGET_XY = (3, 3)

INNER_PAIRS = [(i, k) for i in range(DATES) for k in range(LAG) if i + k + 1 < DATES]
OUTER_PAIRS = [(i, k) for i in range(DATES) for k in range(LAG) if i + k + 1 >= DATES]
OUTER_FIRST = min(i for i, _ in OUTER_PAIRS)

VMEM = pl.BlockSpec(memory_space=pltpu.VMEM)
SMEM = pl.BlockSpec(memory_space=pltpu.SMEM)
ANY = pl.BlockSpec(memory_space=pl.ANY)
PARAMS = pltpu.CompilerParams(vmem_limit_bytes=16 * 1024 * 1024)


def f32(*shape):
    return jax.ShapeDtypeStruct(shape, jnp.float32)


def lane_roll(x, by):
    return pltpu.roll(x, by % x.shape[-1], axis=x.ndim - 1)


def half_swap(x):
    return pltpu.roll(x, LOOKS, axis=0)


def upper(x):
    return lax.broadcasted_iota(jnp.int32, x.shape, 0) < LOOKS


def place(unit):
    n = max(n for n in range(COUNT) if STARTS[n] <= unit)
    return n, unit - STARTS[n]


def masked_tile(buf, first, stop, d, q, j, base):
    row = AZ * (lax.broadcasted_iota(jnp.int32, (8, LANES), 0) % LOOKS) + q
    keep = (row >= first[d]) & (row < stop[d])
    at = base + q * ROW + 2 * j
    tile = jnp.concatenate(
        [buf[pl.ds(at + part, LOOKS, stride=AZ * ROW), :] for part in range(2)], axis=0
    )
    return jnp.where(keep, tile, 0.0)


def load_dates(slc, buf, sems, dates):
    copies = [
        pltpu.make_async_copy(
            slc.at[pl.ds(d * PER_DATE, PER_DATE)],
            buf.at[pl.ds(n * PER_DATE, PER_DATE)],
            sems.at[n],
        )
        for n, d in enumerate(dates)
    ]
    for copy in copies:
        copy.start()
    return copies


def prepare(slc, first, stop, *refs):
    pieces = refs[:COUNT]
    low, edge_low, edge_high, buf, sems = refs[COUNT:]
    copies = load_dates(slc, buf, sems, range(DATES))
    lane = lax.broadcasted_iota(jnp.int32, (8, LANES), 1)
    for d in range(DATES):
        copies[d].wait()
        slot = d % LAG
        for q in range(AZ):
            for j in range(CHUNKS):
                is_edge = j in (0, CHUNKS - 1)
                if d >= LAG and not is_edge:
                    continue
                tile = masked_tile(buf, first, stop, d, q, j, d * PER_DATE)
                if d < LAG:
                    n, at = place(d * AZ + q)
                    lanes = slice(j * LANES, (j + 1) * LANES)
                    pieces[n][at, :, lanes] = tile
                    low[d * AZ + q, :, lanes] = tile
                if is_edge:
                    edge, begin = (edge_low, 0) if j == 0 else (edge_high, -SLOT // 2)
                    here = (lane - SLOT * slot - begin) % LANES < SLOT // 2
                    rest = 0.0 if slot == 0 else edge[d // LAG, q]
                    edge[d // LAG, q] = jnp.where(here, lane_roll(tile, SLOT * slot), rest)


def lay_out_last(slc, first, stop, high, buf, sems):
    copies = load_dates(slc, buf, sems, range(LAG, DATES))
    for d in range(LAG, DATES):
        copies[d - LAG].wait()
        for q in range(AZ):
            for j in range(CHUNKS):
                high[d - LAG, q, :, j * LANES : (j + 1) * LANES] = masked_tile(
                    buf, first, stop, d, q, j, (d - LAG) * PER_DATE
                )


def halo_of(edges, d):
    return [lane_roll(edges[d // LAG, q], -SLOT * (d % LAG)) for q in range(AZ)]


def products(a, b, b_swapped):
    straight = a[0] * b[0]
    crossed = a[0] * b_swapped[0]
    for q in range(1, AZ):
        straight = straight + a[q] * b[q]
        crossed = crossed + a[q] * b_swapped[q]
    return jnp.where(
        upper(straight), straight + half_swap(straight), crossed - half_swap(crossed)
    )


def power_of(a):
    total = a[0] * a[0]
    for q in range(1, AZ):
        total = total + a[q] * a[q]
    return total + half_swap(total)


def look_sums(sums, pairs, shift, mine, theirs, powered, lanes):
    swapped = {j: [half_swap(t) for t in theirs[j]] for j in {i + k + 1 - shift for i, k in pairs}}
    for n, (i, k) in enumerate(pairs):
        j = i + k + 1 - shift
        sums[8 * n : 8 * n + 8, lanes] = products(mine[i], theirs[j], swapped[j])
    for m in range(len(powered) // 2):
        one, two = power_of(powered[2 * m]), power_of(powered[2 * m + 1])
        at = 8 * (len(pairs) + m)
        sums[at : at + 8, lanes] = jnp.where(upper(one), one, two)


def fill(sums, tiles_at, halo, body):
    body(halo, pl.ds(0, LANES))
    rows = sums.shape[0]
    sums[:, COLS + LANES :] = sums[:, :LANES].reshape(rows, LANES)

    @pl.loop(0, CHUNKS)
    def _(c):
        body(
            tiles_at(pl.ds(pl.multiple_of(c * LANES, LANES), LANES)),
            pl.ds(pl.multiple_of((c + 1) * LANES, LANES), LANES),
        )


def windows(sums, g):
    k = lax.broadcasted_iota(jnp.int32, (2 * GROUP, GROUP), 0) - LANES
    n = lax.broadcasted_iota(jnp.int32, (2 * GROUP, GROUP), 1)
    band = ((k >= n - MARGIN) & (k < n + MARGIN)).astype(jnp.float32).astype(jnp.bfloat16)
    left = sums[:, g * GROUP : (g + 2) * GROUP]
    total = None
    for _ in range(3):
        term = left.astype(jnp.bfloat16)
        left = left - term.astype(jnp.float32)
        part = jnp.dot(term, band, preferred_element_type=jnp.float32)
        total = part if total is None else total + part
    return total


def unpacked_powers(result, base, count):
    powers = []
    for m in range(count // 2):
        both = result[base + 8 * m : base + 8 * m + 8]
        other = half_swap(both)
        powers.append(jnp.where(upper(both), both, other))
        powers.append(jnp.where(upper(both), other, both))
    return powers


def write_pair(store, cross, power_first, power_second, used):
    gamma = cross * (used * lax.rsqrt(jnp.maximum(power_first * power_second, 1.0)))
    square = gamma * gamma
    magnitude = jnp.sqrt(square + half_swap(square))
    store(0, gamma[:LOOKS])
    store(1, gamma[LOOKS:])
    store(2, magnitude[:LOOKS])


def own_tiles(pieces, high, lanes, dates):
    tiles = {}
    for d in dates:
        if d < LAG:
            units = [place(d * AZ + q) for q in range(AZ)]
            tiles[d] = [pieces[n][at, :, lanes] for n, at in units]
        else:
            tiles[d] = [high[d - LAG, q, :, lanes] for q in range(AZ)]
    return tiles


def inner(*refs):
    pieces = refs[:COUNT]
    slc, first, stop, edges, used, out, power, high, sums, buf, sems = refs[COUNT:]
    dates = range(DATES)
    lay_out_last(slc, first, stop, high, buf, sems)

    def body(tiles, lanes):
        powered = [tiles[d] for d in dates]
        look_sums(sums, INNER_PAIRS, 0, tiles, tiles, powered, lanes)

    fill(
        sums,
        lambda lanes: own_tiles(pieces, high, lanes, dates),
        {d: halo_of(edges, d) for d in dates},
        body,
    )
    for g in range(COLS // GROUP):
        lanes = slice(g * GROUP, (g + 1) * GROUP)
        result = windows(sums, g)
        powers = unpacked_powers(result, 8 * len(INNER_PAIRS), DATES)
        for d in range(OUTER_FIRST, DATES):
            power[d - OUTER_FIRST, :, lanes] = powers[d]
        for n, (i, k) in enumerate(INNER_PAIRS):

            def store(m, value, i=i, k=k, lanes=lanes):
                out[i, k, m, :, lanes] = value

            write_pair(
                store,
                result[8 * n : 8 * n + 8],
                powers[i],
                powers[i + k + 1],
                used[i, k].astype(jnp.float32),
            )


def outer(*refs):
    pieces = refs[:COUNT]
    high, edges, power, used, received, their_edges = refs[COUNT : COUNT + 6]
    far = refs[COUNT + 6 : 2 * COUNT + 6]
    out, sums, staged, sems = refs[2 * COUNT + 7 :]
    dates = range(OUTER_FIRST, DATES)

    def body(tiles, lanes):
        mine, theirs = tiles
        look_sums(sums, OUTER_PAIRS, DATES, mine, theirs, theirs, lanes)

    def tiles_at(lanes):
        theirs = []
        for d in range(LAG):
            units = [d * AZ + q for q in range(AZ)]
            theirs.append(
                [
                    received[unit, :, lanes] + far[place(unit)[0]][place(unit)[1], :, lanes]
                    for unit in units
                ]
            )
        return own_tiles(pieces, high, lanes, dates), theirs

    fill(
        sums,
        tiles_at,
        (
            {d: halo_of(edges, d) for d in dates},
            [halo_of(their_edges, d) for d in range(LAG)],
        ),
        body,
    )
    for g in range(COLS // GROUP):
        lanes = slice(g * GROUP, (g + 1) * GROUP)
        result = windows(sums, g)
        powers = unpacked_powers(result, 8 * len(OUTER_PAIRS), LAG)
        for n, (i, k) in enumerate(OUTER_PAIRS):

            def store(m, value, n=n, lanes=lanes):
                staged[n, m, :, lanes] = value

            write_pair(
                store,
                result[8 * n : 8 * n + 8],
                power[i - OUTER_FIRST, :, lanes],
                powers[i + k + 1 - DATES],
                used[i, k].astype(jnp.float32),
            )
    copies = [
        pltpu.make_async_copy(staged.at[n], out.at[i, k], sems.at[n])
        for n, (i, k) in enumerate(OUTER_PAIRS)
    ]
    for copy in copies:
        copy.start()
    for copy in copies:
        copy.wait()


def far_permutes():
    def flat(x, y, z, core):
        return ((z // 8) * 16 + y * 4 + x) * 16 + (z % 8) * 2 + core

    scatter = [[] for _ in PIECES]
    gather = [[] for _ in PIECES]
    for z in range(8):
        for core in range(2):
            for n, (x, y) in enumerate(COLUMN_SETS[z // 2][core]):
                relay = flat(x, y, 8 + z, core)
                scatter[n].append((flat(*SOURCE_XY, 8 + z, core), relay))
                gather[n].append((relay, flat(*TARGET_XY, z, core)))
    return scatter, gather


def sum_rows(pairs, dates):
    return 8 * (len(pairs) + dates // 2)


def on_device(slc, first_row, stop_row, pair_used):
    slc = slc.reshape(DATES, 2, AZ * LOOKS, CHUNKS, LANES).transpose(0, 2, 3, 1, 4)
    slc = slc.reshape(DATES * PER_DATE, LANES)
    piece_shapes = [f32(size, 8, COLS) for size in PIECES]
    edge_shape = f32(2, AZ, 8, LANES)
    *pieces, low, edge_low, edge_high = pl.pallas_call(
        prepare,
        out_shape=piece_shapes + [f32(LAG * AZ, 8, COLS), edge_shape, edge_shape],
        in_specs=[ANY, SMEM, SMEM],
        out_specs=[VMEM] * (COUNT + 3),
        scratch_shapes=[
            pltpu.VMEM((DATES * PER_DATE, LANES), jnp.float32),
            pltpu.SemaphoreType.DMA((DATES,)),
        ],
        name="prepare",
    )(slc, first_row, stop_row)

    def permute(value, pairs):
        return lax.ppermute(value, AXES, pairs)

    near = [
        (d * 16 + c, (d - 1) * 16 + c) for d in range(1, 32) if d != 16 for c in range(16)
    ]
    far = [(16 * 16 + c, 15 * 16 + c) for c in range(16)]
    to_right = [(d * 16 + c, d * 16 + c + 1) for d in range(32) for c in range(15)]
    to_left = [(b, a) for a, b in to_right]
    scatter, gather = far_permutes()

    scattered = [permute(piece, pairs) for piece, pairs in zip(pieces, scatter)]
    left = permute(edge_high, to_right)
    right = permute(edge_low, to_left)
    received = permute(low, near)
    edges, *scattered = lax.optimization_barrier((right + left, *scattered))
    gathered = [permute(piece, pairs) for piece, pairs in zip(scattered, gather)]
    their_edges = permute(edges[:1], near + far)

    out_shape = f32(DATES, LAG, 3, LOOKS, COLS)
    out, power, high = pl.pallas_call(
        inner,
        out_shape=[
            out_shape,
            f32(DATES - OUTER_FIRST, 8, COLS),
            f32(DATES - LAG, AZ, 8, COLS),
        ],
        in_specs=[VMEM] * COUNT + [ANY, SMEM, SMEM, VMEM, SMEM],
        out_specs=[VMEM] * 3,
        scratch_shapes=[
            pltpu.VMEM((sum_rows(INNER_PAIRS, DATES), WIDE), jnp.float32),
            pltpu.VMEM(((DATES - LAG) * PER_DATE, LANES), jnp.float32),
            pltpu.SemaphoreType.DMA((DATES - LAG,)),
        ],
        compiler_params=PARAMS,
        name="inner",
    )(*pieces, slc, first_row, stop_row, edges, pair_used)
    return pl.pallas_call(
        outer,
        out_shape=out_shape,
        in_specs=[VMEM] * (COUNT + 3) + [SMEM] + [VMEM] * (COUNT + 2) + [ANY],
        out_specs=ANY,
        input_output_aliases={2 * COUNT + 6: 0},
        scratch_shapes=[
            pltpu.VMEM((sum_rows(OUTER_PAIRS, LAG), WIDE), jnp.float32),
            pltpu.VMEM((len(OUTER_PAIRS), 3, LOOKS, COLS), jnp.float32),
            pltpu.SemaphoreType.DMA((len(OUTER_PAIRS),)),
        ],
        compiler_params=PARAMS,
        name="outer",
    )(*pieces, high, edges, power, pair_used, received, their_edges, *gathered, out)


def solution(mesh):
    return jax.shard_map(
        on_device,
        mesh=mesh,
        in_specs=(P("date", None, None, "col"), P("date"), P("date"), P("date", None)),
        out_specs=P("date", None, None, None, "col"),
        check_vma=False,
    )
```

```python
import jax
import jax.numpy as jnp
from jax import lax
from jax.experimental import pallas as pl
from jax.experimental.pallas import tpu as pltpu
from jax.sharding import PartitionSpec as P

AZ = 5
LAG = 4
DATES = 6
LOOKS = 4
COLS = 1024
MARGIN = 10
LANES = 128
CHUNKS = COLS // LANES
GROUP = 2 * LANES
ROW = 2 * CHUNKS
PER_DATE = AZ * LOOKS * ROW
WIDE = COLS + 2 * LANES
AXES = ("date", "col")

SLOT = LANES // LAG

PIECES = (10, 10)
COUNT = len(PIECES)
STARTS = [sum(PIECES[:n]) for n in range(COUNT)]
COLUMN_SETS = (
    (((0, 0), (3, 0)), ((0, 3), (3, 3))),
    (((1, 0), (0, 1)), ((2, 3), (3, 2))),
    (((2, 0), (0, 2)), ((1, 3), (3, 1))),
    (((1, 1), (2, 2)), ((2, 1), (1, 2))),
)
SOURCE_XY = (0, 0)
TARGET_XY = (3, 3)

INNER_PAIRS = [(i, k) for i in range(DATES) for k in range(LAG) if i + k + 1 < DATES]
OUTER_PAIRS = [(i, k) for i in range(DATES) for k in range(LAG) if i + k + 1 >= DATES]
OUTER_FIRST = min(i for i, _ in OUTER_PAIRS)

VMEM = pl.BlockSpec(memory_space=pltpu.VMEM)
SMEM = pl.BlockSpec(memory_space=pltpu.SMEM)
ANY = pl.BlockSpec(memory_space=pl.ANY)
PARAMS = pltpu.CompilerParams(vmem_limit_bytes=16 * 1024 * 1024)


def f32(*shape):
    return jax.ShapeDtypeStruct(shape, jnp.float32)


def f32_vmem(*shape):
    return pltpu.VMEM(shape, jnp.float32)


def in_hbm(x):
    return pltpu.with_memory_space_constraint(x, pltpu.HBM)


def lane_roll(x, by):
    return pltpu.roll(x, by % x.shape[-1], axis=x.ndim - 1)


def half_swap(x):
    return pltpu.roll(x, LOOKS, axis=0)


def upper(x):
    return lax.broadcasted_iota(jnp.int32, x.shape, 0) < LOOKS


def place(unit):
    n = max(n for n in range(COUNT) if STARTS[n] <= unit)
    return n, unit - STARTS[n]


def masked_tile(buf, first, stop, d, q, j, base):
    row = AZ * (lax.broadcasted_iota(jnp.int32, (8, LANES), 0) % LOOKS) + q
    keep = (row >= first[d]) & (row < stop[d])
    at = base + q * ROW + 2 * j
    tile = jnp.concatenate(
        [buf[pl.ds(at + part, LOOKS, stride=AZ * ROW), :] for part in range(2)], axis=0
    )
    return jnp.where(keep, tile, 0.0)


def load_dates(slc, buf, sems, dates):
    copies = [
        pltpu.make_async_copy(
            slc.at[pl.ds(d * PER_DATE, PER_DATE)],
            buf.at[pl.ds(n * PER_DATE, PER_DATE)],
            sems.at[n],
        )
        for n, d in enumerate(dates)
    ]
    for copy in copies:
        copy.start()
    return copies


def prepare(slc, first, stop, *refs):
    pieces = refs[:COUNT]
    low, edge_low, edge_high, buf, sems = refs[COUNT:]
    copies = load_dates(slc, buf, sems, range(DATES))
    lane = lax.broadcasted_iota(jnp.int32, (8, LANES), 1)
    for d in range(DATES):
        copies[d].wait()
        slot = d % LAG
        for q in range(AZ):
            for j in range(CHUNKS):
                is_edge = j in (0, CHUNKS - 1)
                if d >= LAG and not is_edge:
                    continue
                tile = masked_tile(buf, first, stop, d, q, j, d * PER_DATE)
                if d < LAG:
                    n, at = place(d * AZ + q)
                    lanes = slice(j * LANES, (j + 1) * LANES)
                    pieces[n][at, :, lanes] = tile
                    low[d * AZ + q, :, lanes] = tile
                if is_edge:
                    edge, begin = (edge_low, 0) if j == 0 else (edge_high, -SLOT // 2)
                    here = (lane - SLOT * slot - begin) % LANES < SLOT // 2
                    rest = 0.0 if slot == 0 else edge[d // LAG, q]
                    edge[d // LAG, q] = jnp.where(here, lane_roll(tile, SLOT * slot), rest)


def lay_out_last(slc, first, stop, high, buf, sems):
    copies = load_dates(slc, buf, sems, range(LAG, DATES))
    for d in range(LAG, DATES):
        copies[d - LAG].wait()
        for q in range(AZ):
            for j in range(CHUNKS):
                high[d - LAG, q, :, j * LANES : (j + 1) * LANES] = masked_tile(
                    buf, first, stop, d, q, j, (d - LAG) * PER_DATE
                )


def halo_of(edges, d):
    return [lane_roll(edges[d // LAG, q], -SLOT * (d % LAG)) for q in range(AZ)]


def products(a, b, b_swapped):
    straight = a[0] * b[0]
    crossed = a[0] * b_swapped[0]
    for q in range(1, AZ):
        straight = straight + a[q] * b[q]
        crossed = crossed + a[q] * b_swapped[q]
    return jnp.where(
        upper(straight), straight + half_swap(straight), crossed - half_swap(crossed)
    )


def power_of(a):
    total = a[0] * a[0]
    for q in range(1, AZ):
        total = total + a[q] * a[q]
    return total + half_swap(total)


def look_sums(sums, pairs, shift, mine, theirs, powered, lanes):
    swapped = {j: [half_swap(t) for t in theirs[j]] for j in {i + k + 1 - shift for i, k in pairs}}
    for n, (i, k) in enumerate(pairs):
        j = i + k + 1 - shift
        sums[8 * n : 8 * n + 8, lanes] = products(mine[i], theirs[j], swapped[j])
    for m in range(len(powered) // 2):
        one, two = power_of(powered[2 * m]), power_of(powered[2 * m + 1])
        at = 8 * (len(pairs) + m)
        sums[at : at + 8, lanes] = jnp.where(upper(one), one, two)


def fill(sums, tiles_at, halo, body):
    body(halo, pl.ds(0, LANES))
    rows = sums.shape[0]
    sums[:, COLS + LANES :] = sums[:, :LANES].reshape(rows, LANES)

    @pl.loop(0, CHUNKS)
    def _(c):
        body(
            tiles_at(pl.ds(pl.multiple_of(c * LANES, LANES), LANES)),
            pl.ds(pl.multiple_of((c + 1) * LANES, LANES), LANES),
        )


def windows(sums, g):
    k = lax.broadcasted_iota(jnp.int32, (2 * GROUP, GROUP), 0) - LANES
    n = lax.broadcasted_iota(jnp.int32, (2 * GROUP, GROUP), 1)
    band = ((k >= n - MARGIN) & (k < n + MARGIN)).astype(jnp.float32).astype(jnp.bfloat16)
    left = sums[:, g * GROUP : (g + 2) * GROUP]
    total = None
    for _ in range(3):
        term = left.astype(jnp.bfloat16)
        left = left - term.astype(jnp.float32)
        part = jnp.dot(term, band, preferred_element_type=jnp.float32)
        total = part if total is None else total + part
    return total


def unpacked_powers(result, base, count):
    powers = []
    for m in range(count // 2):
        both = result[base + 8 * m : base + 8 * m + 8]
        other = half_swap(both)
        powers.append(jnp.where(upper(both), both, other))
        powers.append(jnp.where(upper(both), other, both))
    return powers


def write_pair(store, cross, power_first, power_second, used):
    gamma = cross * (used * lax.rsqrt(jnp.maximum(power_first * power_second, 1.0)))
    square = gamma * gamma
    magnitude = jnp.sqrt(square + half_swap(square))
    store(0, gamma[:LOOKS])
    store(1, gamma[LOOKS:])
    store(2, magnitude[:LOOKS])


def own_tiles(pieces, high, lanes, dates):
    tiles = {}
    for d in dates:
        if d < LAG:
            units = [place(d * AZ + q) for q in range(AZ)]
            tiles[d] = [pieces[n][at, :, lanes] for n, at in units]
        else:
            tiles[d] = [high[d - LAG, q, :, lanes] for q in range(AZ)]
    return tiles


def inner(*refs):
    pieces = refs[:COUNT]
    slc, first, stop, edges, used, out, power, high, sums, buf, sems = refs[COUNT:]
    dates = range(DATES)
    lay_out_last(slc, first, stop, high, buf, sems)

    def body(tiles, lanes):
        powered = [tiles[d] for d in dates]
        look_sums(sums, INNER_PAIRS, 0, tiles, tiles, powered, lanes)

    fill(
        sums,
        lambda lanes: own_tiles(pieces, high, lanes, dates),
        {d: halo_of(edges, d) for d in dates},
        body,
    )
    for g in range(COLS // GROUP):
        lanes = slice(g * GROUP, (g + 1) * GROUP)
        result = windows(sums, g)
        powers = unpacked_powers(result, 8 * len(INNER_PAIRS), DATES)
        for d in range(OUTER_FIRST, DATES):
            power[d - OUTER_FIRST, :, lanes] = powers[d]
        for n, (i, k) in enumerate(INNER_PAIRS):

            def store(m, value, i=i, k=k, lanes=lanes):
                out[i, k, m, :, lanes] = value

            write_pair(
                store,
                result[8 * n : 8 * n + 8],
                powers[i],
                powers[i + k + 1],
                used[k, i].astype(jnp.float32),
            )


def outer(*refs):
    pieces = refs[:COUNT]
    high, edges, power, used, received, their_edges = refs[COUNT : COUNT + 6]
    far = refs[COUNT + 6 : 2 * COUNT + 6]
    out, sums, staged, sems = refs[2 * COUNT + 7 :]
    dates = range(OUTER_FIRST, DATES)

    def body(tiles, lanes):
        mine, theirs = tiles
        look_sums(sums, OUTER_PAIRS, DATES, mine, theirs, theirs, lanes)

    def tiles_at(lanes):
        theirs = []
        for d in range(LAG):
            units = [d * AZ + q for q in range(AZ)]
            theirs.append(
                [
                    received[unit, :, lanes] + far[place(unit)[0]][place(unit)[1], :, lanes]
                    for unit in units
                ]
            )
        return own_tiles(pieces, high, lanes, dates), theirs

    fill(
        sums,
        tiles_at,
        (
            {d: halo_of(edges, d) for d in dates},
            [halo_of(their_edges, d) for d in range(LAG)],
        ),
        body,
    )
    for g in range(COLS // GROUP):
        lanes = slice(g * GROUP, (g + 1) * GROUP)
        result = windows(sums, g)
        powers = unpacked_powers(result, 8 * len(OUTER_PAIRS), LAG)
        for n, (i, k) in enumerate(OUTER_PAIRS):

            def store(m, value, n=n, lanes=lanes):
                staged[n, m, :, lanes] = value

            write_pair(
                store,
                result[8 * n : 8 * n + 8],
                power[i - OUTER_FIRST, :, lanes],
                powers[i + k + 1 - DATES],
                used[k, i].astype(jnp.float32),
            )
    copies = [
        pltpu.make_async_copy(staged.at[n], out.at[i, k], sems.at[n])
        for n, (i, k) in enumerate(OUTER_PAIRS)
    ]
    for copy in copies:
        copy.start()
    for copy in copies:
        copy.wait()


def far_permutes():
    def flat(x, y, z, core):
        return ((z // 8) * 16 + y * 4 + x) * 16 + (z % 8) * 2 + core

    scatter = [[] for _ in PIECES]
    gather = [[] for _ in PIECES]
    for z in range(8):
        for core in range(2):
            for n, (x, y) in enumerate(COLUMN_SETS[z // 2][core]):
                relay = flat(x, y, 8 + z, core)
                scatter[n].append((flat(*SOURCE_XY, 8 + z, core), relay))
                gather[n].append((relay, flat(*TARGET_XY, z, core)))
    return scatter, gather


def sum_rows(pairs, dates):
    return 8 * (len(pairs) + dates // 2)


def on_device(slc, first_row, stop_row, pair_used):
    slc = slc.reshape(DATES, 2, AZ * LOOKS, CHUNKS, LANES).transpose(0, 2, 3, 1, 4)
    slc = slc.reshape(DATES * PER_DATE, LANES)
    piece_shapes = [f32_vmem(size, 8, COLS) for size in PIECES]
    edge_shape = f32_vmem(2, AZ, 8, LANES)
    *pieces, low, edge_low, edge_high = pl.pallas_call(
        prepare,
        out_shape=piece_shapes + [f32_vmem(LAG * AZ, 8, COLS), edge_shape, edge_shape],
        in_specs=[ANY, SMEM, SMEM],
        out_specs=[VMEM] * (COUNT + 3),
        scratch_shapes=[
            pltpu.VMEM((DATES * PER_DATE, LANES), jnp.float32),
            pltpu.SemaphoreType.DMA((DATES,)),
        ],
        compiler_params=PARAMS,
        name="prepare",
    )(in_hbm(slc), in_hbm(first_row), in_hbm(stop_row))

    def permute(value, pairs):
        return lax.ppermute(value, AXES, pairs)

    near = [
        (d * 16 + c, (d - 1) * 16 + c) for d in range(1, 32) if d != 16 for c in range(16)
    ]
    far = [(16 * 16 + c, 15 * 16 + c) for c in range(16)]
    to_right = [(d * 16 + c, d * 16 + c + 1) for d in range(32) for c in range(15)]
    to_left = [(b, a) for a, b in to_right]
    scatter, gather = far_permutes()

    scattered = [permute(piece, pairs) for piece, pairs in zip(pieces, scatter)]
    left = permute(edge_high, to_right)
    right = permute(edge_low, to_left)
    received = permute(low, near)
    edges = right + left
    gathered = [permute(piece, pairs) for piece, pairs in zip(scattered, gather)]
    their_edges = permute(edges[:1], near + far)

    used = pair_used.T
    out_shape = f32(DATES, LAG, 3, LOOKS, COLS)
    out, power, high = pl.pallas_call(
        inner,
        out_shape=[
            out_shape,
            f32_vmem(DATES - OUTER_FIRST, 8, COLS),
            f32_vmem(DATES - LAG, AZ, 8, COLS),
        ],
        in_specs=[VMEM] * COUNT + [ANY, SMEM, SMEM, VMEM, SMEM],
        out_specs=[VMEM] * 3,
        scratch_shapes=[
            pltpu.VMEM((sum_rows(INNER_PAIRS, DATES), WIDE), jnp.float32),
            pltpu.VMEM(((DATES - LAG) * PER_DATE, LANES), jnp.float32),
            pltpu.SemaphoreType.DMA((DATES - LAG,)),
        ],
        compiler_params=PARAMS,
        name="inner",
    )(*pieces, in_hbm(slc), in_hbm(first_row), in_hbm(stop_row), edges, in_hbm(used))
    return pl.pallas_call(
        outer,
        out_shape=out_shape,
        in_specs=[VMEM] * (COUNT + 3) + [SMEM] + [VMEM] * (COUNT + 2) + [ANY],
        out_specs=ANY,
        input_output_aliases={2 * COUNT + 6: 0},
        scratch_shapes=[
            pltpu.VMEM((sum_rows(OUTER_PAIRS, LAG), WIDE), jnp.float32),
            pltpu.VMEM((len(OUTER_PAIRS), 3, LOOKS, COLS), jnp.float32),
            pltpu.SemaphoreType.DMA((len(OUTER_PAIRS),)),
        ],
        compiler_params=PARAMS,
        name="outer",
    )(*pieces, high, edges, power, in_hbm(used), received, their_edges, *gathered, out)


def solution(mesh):
    return jax.shard_map(
        on_device,
        mesh=mesh,
        in_specs=(P("date", None, None, "col"), P("date"), P("date"), P("date", None)),
        out_specs=P("date", None, None, None, "col"),
        check_vma=False,
    )
```

```python
import jax
import jax.numpy as jnp
from jax import lax
from jax.experimental import pallas as pl
from jax.experimental.pallas import tpu as pltpu
from jax.sharding import PartitionSpec as P

AZ = 5
LAG = 4
DATES = 6
LOOKS = 4
COLS = 1024
MARGIN = 10
LANES = 128
CHUNKS = COLS // LANES
GROUP = 2 * LANES
ROW = 2 * CHUNKS
PER_DATE = AZ * LOOKS * ROW
WIDE = COLS + 2 * LANES
AXES = ("date", "col")

SLOT = LANES // LAG

PIECES = (10, 10)
COUNT = len(PIECES)
STARTS = [sum(PIECES[:n]) for n in range(COUNT)]
COLUMN_SETS = (
    (None, ((3, 0), (1, 3))),
    (((0, 3), (3, 1)), ((1, 0), (0, 1))),
    (((0, 1), (1, 0)), ((2, 0), (0, 3))),
    (((0, 2), (3, 0)), ((1, 1), (2, 0))),
)
SOURCE_XY = (0, 0)
TARGET_XY = (3, 3)

INNER_PAIRS = [(i, k) for i in range(DATES) for k in range(LAG) if i + k + 1 < DATES]
OUTER_PAIRS = [(i, k) for i in range(DATES) for k in range(LAG) if i + k + 1 >= DATES]
OUTER_FIRST = min(i for i, _ in OUTER_PAIRS)

VMEM = pl.BlockSpec(memory_space=pltpu.VMEM)
SMEM = pl.BlockSpec(memory_space=pltpu.SMEM)
ANY = pl.BlockSpec(memory_space=pl.ANY)
PARAMS = pltpu.CompilerParams(vmem_limit_bytes=16 * 1024 * 1024)


def f32(*shape):
    return jax.ShapeDtypeStruct(shape, jnp.float32)


def f32_vmem(*shape):
    return pltpu.VMEM(shape, jnp.float32)


def in_hbm(x):
    return pltpu.with_memory_space_constraint(x, pltpu.HBM)


def lane_roll(x, by):
    return pltpu.roll(x, by % x.shape[-1], axis=x.ndim - 1)


def half_swap(x):
    return pltpu.roll(x, LOOKS, axis=0)


def upper(x):
    return lax.broadcasted_iota(jnp.int32, x.shape, 0) < LOOKS


def place(unit):
    n = max(n for n in range(COUNT) if STARTS[n] <= unit)
    return n, unit - STARTS[n]


def masked_tile(buf, first, stop, d, q, j, base):
    row = AZ * (lax.broadcasted_iota(jnp.int32, (8, LANES), 0) % LOOKS) + q
    keep = (row >= first[d]) & (row < stop[d])
    at = base + q * ROW + 2 * j
    tile = jnp.concatenate(
        [buf[pl.ds(at + part, LOOKS, stride=AZ * ROW), :] for part in range(2)], axis=0
    )
    return jnp.where(keep, tile, 0.0)


def load_dates(slc, buf, sems, dates):
    copies = [
        pltpu.make_async_copy(
            slc.at[pl.ds(d * PER_DATE, PER_DATE)],
            buf.at[pl.ds(n * PER_DATE, PER_DATE)],
            sems.at[n],
        )
        for n, d in enumerate(dates)
    ]
    for copy in copies:
        copy.start()
    return copies


def prepare(slc, first, stop, *refs):
    pieces = refs[:COUNT]
    low, edge_low, edge_high, buf, sems = refs[COUNT:]
    copies = load_dates(slc, buf, sems, range(DATES))
    lane = lax.broadcasted_iota(jnp.int32, (8, LANES), 1)
    for d in range(DATES):
        copies[d].wait()
        slot = d % LAG
        for q in range(AZ):
            for j in range(CHUNKS):
                is_edge = j in (0, CHUNKS - 1)
                if d >= LAG and not is_edge:
                    continue
                tile = masked_tile(buf, first, stop, d, q, j, d * PER_DATE)
                if d < LAG:
                    n, at = place(d * AZ + q)
                    lanes = slice(j * LANES, (j + 1) * LANES)
                    pieces[n][at, :, lanes] = tile
                    low[d * AZ + q, :, lanes] = tile
                if is_edge:
                    edge, begin = (edge_low, 0) if j == 0 else (edge_high, -SLOT // 2)
                    here = (lane - SLOT * slot - begin) % LANES < SLOT // 2
                    rest = 0.0 if slot == 0 else edge[d // LAG, q]
                    edge[d // LAG, q] = jnp.where(here, lane_roll(tile, SLOT * slot), rest)


def lay_out_last(slc, first, stop, high, buf, sems):
    copies = load_dates(slc, buf, sems, range(LAG, DATES))
    for d in range(LAG, DATES):
        copies[d - LAG].wait()
        for q in range(AZ):
            for j in range(CHUNKS):
                high[d - LAG, q, :, j * LANES : (j + 1) * LANES] = masked_tile(
                    buf, first, stop, d, q, j, (d - LAG) * PER_DATE
                )


def halo_of(edges, d):
    return [lane_roll(edges[d // LAG, q], -SLOT * (d % LAG)) for q in range(AZ)]


def products(a, b, b_swapped):
    straight = a[0] * b[0]
    crossed = a[0] * b_swapped[0]
    for q in range(1, AZ):
        straight = straight + a[q] * b[q]
        crossed = crossed + a[q] * b_swapped[q]
    return jnp.where(
        upper(straight), straight + half_swap(straight), crossed - half_swap(crossed)
    )


def power_of(a):
    total = a[0] * a[0]
    for q in range(1, AZ):
        total = total + a[q] * a[q]
    return total + half_swap(total)


def look_sums(sums, pairs, shift, mine, theirs, powered, lanes):
    swapped = {j: [half_swap(t) for t in theirs[j]] for j in {i + k + 1 - shift for i, k in pairs}}
    for n, (i, k) in enumerate(pairs):
        j = i + k + 1 - shift
        sums[8 * n : 8 * n + 8, lanes] = products(mine[i], theirs[j], swapped[j])
    for m in range(len(powered) // 2):
        one, two = power_of(powered[2 * m]), power_of(powered[2 * m + 1])
        at = 8 * (len(pairs) + m)
        sums[at : at + 8, lanes] = jnp.where(upper(one), one, two)


def fill(sums, tiles_at, halo, body):
    body(halo, pl.ds(0, LANES))
    rows = sums.shape[0]
    sums[:, COLS + LANES :] = sums[:, :LANES].reshape(rows, LANES)

    @pl.loop(0, CHUNKS)
    def _(c):
        body(
            tiles_at(pl.ds(pl.multiple_of(c * LANES, LANES), LANES)),
            pl.ds(pl.multiple_of((c + 1) * LANES, LANES), LANES),
        )


def windows(sums, g):
    k = lax.broadcasted_iota(jnp.int32, (2 * GROUP, GROUP), 0) - LANES
    n = lax.broadcasted_iota(jnp.int32, (2 * GROUP, GROUP), 1)
    band = ((k >= n - MARGIN) & (k < n + MARGIN)).astype(jnp.float32).astype(jnp.bfloat16)
    left = sums[:, g * GROUP : (g + 2) * GROUP]
    total = None
    for _ in range(3):
        term = left.astype(jnp.bfloat16)
        left = left - term.astype(jnp.float32)
        part = jnp.dot(term, band, preferred_element_type=jnp.float32)
        total = part if total is None else total + part
    return total


def unpacked_powers(result, base, count):
    powers = []
    for m in range(count // 2):
        both = result[base + 8 * m : base + 8 * m + 8]
        other = half_swap(both)
        powers.append(jnp.where(upper(both), both, other))
        powers.append(jnp.where(upper(both), other, both))
    return powers


def write_pair(store, cross, power_first, power_second, used):
    gamma = cross * (used * lax.rsqrt(jnp.maximum(power_first * power_second, 1.0)))
    square = gamma * gamma
    magnitude = jnp.sqrt(square + half_swap(square))
    store(0, gamma[:LOOKS])
    store(1, gamma[LOOKS:])
    store(2, magnitude[:LOOKS])


def own_tiles(pieces, high, lanes, dates):
    tiles = {}
    for d in dates:
        if d < LAG:
            units = [place(d * AZ + q) for q in range(AZ)]
            tiles[d] = [pieces[n][at, :, lanes] for n, at in units]
        else:
            tiles[d] = [high[d - LAG, q, :, lanes] for q in range(AZ)]
    return tiles


def inner(*refs):
    pieces = refs[:COUNT]
    slc, first, stop, edges, used, out, power, high, sums, buf, sems = refs[COUNT:]
    dates = range(DATES)
    lay_out_last(slc, first, stop, high, buf, sems)

    def body(tiles, lanes):
        powered = [tiles[d] for d in dates]
        look_sums(sums, INNER_PAIRS, 0, tiles, tiles, powered, lanes)

    fill(
        sums,
        lambda lanes: own_tiles(pieces, high, lanes, dates),
        {d: halo_of(edges, d) for d in dates},
        body,
    )
    for g in range(COLS // GROUP):
        lanes = slice(g * GROUP, (g + 1) * GROUP)
        result = windows(sums, g)
        powers = unpacked_powers(result, 8 * len(INNER_PAIRS), DATES)
        for d in range(OUTER_FIRST, DATES):
            power[d - OUTER_FIRST, :, lanes] = powers[d]
        for n, (i, k) in enumerate(INNER_PAIRS):

            def store(m, value, i=i, k=k, lanes=lanes):
                out[i, k, m, :, lanes] = value

            write_pair(
                store,
                result[8 * n : 8 * n + 8],
                powers[i],
                powers[i + k + 1],
                used[k, i].astype(jnp.float32),
            )


def outer(*refs):
    pieces = refs[:COUNT]
    high, edges, power, used, received, their_edges = refs[COUNT : COUNT + 6]
    far = refs[COUNT + 6 : 2 * COUNT + 6]
    out, sums, staged, sems = refs[2 * COUNT + 7 :]
    dates = range(OUTER_FIRST, DATES)

    def body(tiles, lanes):
        mine, theirs = tiles
        look_sums(sums, OUTER_PAIRS, DATES, mine, theirs, theirs, lanes)

    def tiles_at(lanes):
        theirs = []
        for d in range(LAG):
            units = [d * AZ + q for q in range(AZ)]
            theirs.append(
                [
                    received[unit, :, lanes] + far[place(unit)[0]][place(unit)[1], :, lanes]
                    for unit in units
                ]
            )
        return own_tiles(pieces, high, lanes, dates), theirs

    fill(
        sums,
        tiles_at,
        (
            {d: halo_of(edges, d) for d in dates},
            [halo_of(their_edges, d) for d in range(LAG)],
        ),
        body,
    )
    for g in range(COLS // GROUP):
        lanes = slice(g * GROUP, (g + 1) * GROUP)
        result = windows(sums, g)
        powers = unpacked_powers(result, 8 * len(OUTER_PAIRS), LAG)
        for n, (i, k) in enumerate(OUTER_PAIRS):

            def store(m, value, n=n, lanes=lanes):
                staged[n, m, :, lanes] = value

            write_pair(
                store,
                result[8 * n : 8 * n + 8],
                power[i - OUTER_FIRST, :, lanes],
                powers[i + k + 1 - DATES],
                used[k, i].astype(jnp.float32),
            )
    copies = [
        pltpu.make_async_copy(staged.at[n], out.at[i, k], sems.at[n])
        for n, (i, k) in enumerate(OUTER_PAIRS)
    ]
    for copy in copies:
        copy.start()
    for copy in copies:
        copy.wait()


def far_permutes():
    def flat(x, y, z, core):
        return ((z // 8) * 16 + y * 4 + x) * 16 + (z % 8) * 2 + core

    straight = []
    scatter = [[] for _ in PIECES]
    gather = [[] for _ in PIECES]
    for z in range(8):
        for core in range(2):
            if COLUMN_SETS[z // 2][core] is None:
                straight.append((flat(*SOURCE_XY, 8 + z, core), flat(*TARGET_XY, z, core)))
                continue
            for n, (x, y) in enumerate(COLUMN_SETS[z // 2][core]):
                relay = flat(x, y, 8 + z, core)
                scatter[n].append((flat(*SOURCE_XY, 8 + z, core), relay))
                gather[n].append((relay, flat(*TARGET_XY, z, core)))
    return straight, scatter, gather


def sum_rows(pairs, dates):
    return 8 * (len(pairs) + dates // 2)


def on_device(slc, first_row, stop_row, pair_used):
    slc = slc.reshape(DATES, 2, AZ * LOOKS, CHUNKS, LANES).transpose(0, 2, 3, 1, 4)
    slc = slc.reshape(DATES * PER_DATE, LANES)
    piece_shapes = [f32_vmem(size, 8, COLS) for size in PIECES]
    edge_shape = f32_vmem(2, AZ, 8, LANES)
    *pieces, low, edge_low, edge_high = pl.pallas_call(
        prepare,
        out_shape=piece_shapes + [f32_vmem(LAG * AZ, 8, COLS), edge_shape, edge_shape],
        in_specs=[ANY, SMEM, SMEM],
        out_specs=[VMEM] * (COUNT + 3),
        scratch_shapes=[
            pltpu.VMEM((DATES * PER_DATE, LANES), jnp.float32),
            pltpu.SemaphoreType.DMA((DATES,)),
        ],
        compiler_params=PARAMS,
        name="prepare",
    )(in_hbm(slc), in_hbm(first_row), in_hbm(stop_row))

    def permute(value, pairs):
        return lax.ppermute(value, AXES, pairs)

    near = [
        (d * 16 + c, (d - 1) * 16 + c) for d in range(1, 32) if d != 16 for c in range(16)
    ]
    far = [(16 * 16 + c, 15 * 16 + c) for c in range(16)]
    to_right = [(d * 16 + c, d * 16 + c + 1) for d in range(32) for c in range(15)]
    to_left = [(b, a) for a, b in to_right]
    straight, scatter, gather = far_permutes()

    scattered = [permute(piece, pairs) for piece, pairs in zip(pieces, scatter)]
    left = permute(edge_high, to_right)
    right = permute(edge_low, to_left)
    received = permute(low, near + straight)
    edges = right + left
    gathered = [permute(piece, pairs) for piece, pairs in zip(scattered, gather)]
    their_edges = permute(edges[:1], near + far)

    used = pair_used.T
    out_shape = f32(DATES, LAG, 3, LOOKS, COLS)
    out, power, high = pl.pallas_call(
        inner,
        out_shape=[
            out_shape,
            f32_vmem(DATES - OUTER_FIRST, 8, COLS),
            f32_vmem(DATES - LAG, AZ, 8, COLS),
        ],
        in_specs=[VMEM] * COUNT + [ANY, SMEM, SMEM, VMEM, SMEM],
        out_specs=[VMEM] * 3,
        scratch_shapes=[
            pltpu.VMEM((sum_rows(INNER_PAIRS, DATES), WIDE), jnp.float32),
            pltpu.VMEM(((DATES - LAG) * PER_DATE, LANES), jnp.float32),
            pltpu.SemaphoreType.DMA((DATES - LAG,)),
        ],
        compiler_params=PARAMS,
        name="inner",
    )(*pieces, in_hbm(slc), in_hbm(first_row), in_hbm(stop_row), edges, in_hbm(used))
    return pl.pallas_call(
        outer,
        out_shape=out_shape,
        in_specs=[VMEM] * (COUNT + 3) + [SMEM] + [VMEM] * (COUNT + 2) + [ANY],
        out_specs=ANY,
        input_output_aliases={2 * COUNT + 6: 0},
        scratch_shapes=[
            pltpu.VMEM((sum_rows(OUTER_PAIRS, LAG), WIDE), jnp.float32),
            pltpu.VMEM((len(OUTER_PAIRS), 3, LOOKS, COLS), jnp.float32),
            pltpu.SemaphoreType.DMA((len(OUTER_PAIRS),)),
        ],
        compiler_params=PARAMS,
        name="outer",
    )(*pieces, high, edges, power, in_hbm(used), received, their_edges, *gathered, out)


def solution(mesh):
    return jax.shard_map(
        on_device,
        mesh=mesh,
        in_specs=(P("date", None, None, "col"), P("date"), P("date"), P("date", None)),
        out_specs=P("date", None, None, None, "col"),
        check_vma=False,
    )
```

```python
import jax
import jax.numpy as jnp
from jax import lax
from jax.experimental import pallas as pl
from jax.experimental.pallas import tpu as pltpu
from jax.sharding import PartitionSpec as P

AZ = 5
LAG = 4
DATES = 6
LOOKS = 4
COLS = 1024
MARGIN = 10
LANES = 128
CHUNKS = COLS // LANES
GROUP = 2 * LANES
ROW = 2 * CHUNKS
PER_DATE = AZ * LOOKS * ROW
WIDE = COLS + 2 * LANES
AXES = ("date", "col")

SLOT = LANES // LAG

PIECES = (10, 10)
COUNT = len(PIECES)
STARTS = [sum(PIECES[:n]) for n in range(COUNT)]
COLUMN_SETS = (
    (None, ((3, 0), (1, 3))),
    (((0, 3), (3, 1)), ((1, 0), (0, 1))),
    (((1, 1), (0, 3)), ((0, 2), (1, 2))),
    (((0, 1), (3, 0)), ((2, 0), (0, 2))),
)
SOURCE_XY = (0, 0)
TARGET_XY = (3, 3)

INNER_PAIRS = [(i, k) for i in range(DATES) for k in range(LAG) if i + k + 1 < DATES]
OUTER_PAIRS = [(i, k) for i in range(DATES) for k in range(LAG) if i + k + 1 >= DATES]
OUTER_FIRST = min(i for i, _ in OUTER_PAIRS)

VMEM = pl.BlockSpec(memory_space=pltpu.VMEM)
SMEM = pl.BlockSpec(memory_space=pltpu.SMEM)
ANY = pl.BlockSpec(memory_space=pl.ANY)
PARAMS = pltpu.CompilerParams(vmem_limit_bytes=16 * 1024 * 1024)


def f32(*shape):
    return jax.ShapeDtypeStruct(shape, jnp.float32)


def f32_vmem(*shape):
    return pltpu.VMEM(shape, jnp.float32)


def in_hbm(x):
    return pltpu.with_memory_space_constraint(x, pltpu.HBM)


def lane_roll(x, by):
    return pltpu.roll(x, by % x.shape[-1], axis=x.ndim - 1)


def half_swap(x):
    return pltpu.roll(x, LOOKS, axis=0)


def upper(x):
    return lax.broadcasted_iota(jnp.int32, x.shape, 0) < LOOKS


def place(unit):
    n = max(n for n in range(COUNT) if STARTS[n] <= unit)
    return n, unit - STARTS[n]


def valid_rows(first, stop, d, q):
    row = AZ * (lax.broadcasted_iota(jnp.int32, (8, LANES), 0) % LOOKS) + q
    return (row >= first[d]) & (row < stop[d])


def masked_tile(buf, keep, q, j, base):
    at = base + q * ROW + 2 * j
    tile = jnp.concatenate(
        [buf[pl.ds(at + part, LOOKS, stride=AZ * ROW), :] for part in range(2)], axis=0
    )
    return jnp.where(keep, tile, 0.0)


def load_dates(slc, buf, sems, dates):
    copies = [
        pltpu.make_async_copy(
            slc.at[pl.ds(d * PER_DATE, PER_DATE)],
            buf.at[pl.ds(n * PER_DATE, PER_DATE)],
            sems.at[n],
        )
        for n, d in enumerate(dates)
    ]
    for copy in copies:
        copy.start()
    return copies


def prepare(slc, first, stop, *refs):
    pieces = refs[:COUNT]
    low, edge_low, edge_high, buf, sems = refs[COUNT:]
    copies = load_dates(slc, buf, sems, range(DATES))
    lane = lax.broadcasted_iota(jnp.int32, (8, LANES), 1)
    for d in range(DATES):
        copies[d].wait()
        slot = d % LAG
        for q in range(AZ):
            keep = valid_rows(first, stop, d, q)
            for j in range(CHUNKS):
                is_edge = j in (0, CHUNKS - 1)
                if d >= LAG and not is_edge:
                    continue
                tile = masked_tile(buf, keep, q, j, d * PER_DATE)
                if d < LAG:
                    n, at = place(d * AZ + q)
                    lanes = slice(j * LANES, (j + 1) * LANES)
                    pieces[n][at, :, lanes] = tile
                    low[d * AZ + q, :, lanes] = tile
                if is_edge:
                    edge, begin = (edge_low, 0) if j == 0 else (edge_high, -SLOT // 2)
                    here = (lane - SLOT * slot - begin) % LANES < SLOT // 2
                    rest = 0.0 if slot == 0 else edge[d // LAG, q]
                    edge[d // LAG, q] = jnp.where(here, lane_roll(tile, SLOT * slot), rest)


def lay_out_last(slc, first, stop, high, buf, sems):
    copies = load_dates(slc, buf, sems, range(LAG, DATES))
    for d in range(LAG, DATES):
        copies[d - LAG].wait()
        for q in range(AZ):
            keep = valid_rows(first, stop, d, q)
            for j in range(CHUNKS):
                high[d - LAG, q, :, j * LANES : (j + 1) * LANES] = masked_tile(
                    buf, keep, q, j, (d - LAG) * PER_DATE
                )


def halo_of(edges, d):
    return [lane_roll(edges[d // LAG, q], -SLOT * (d % LAG)) for q in range(AZ)]


def products(a, b, b_swapped):
    straight = a[0] * b[0]
    crossed = a[0] * b_swapped[0]
    for q in range(1, AZ):
        straight = straight + a[q] * b[q]
        crossed = crossed + a[q] * b_swapped[q]
    return jnp.where(
        upper(straight), straight + half_swap(straight), crossed - half_swap(crossed)
    )


def power_of(a):
    total = a[0] * a[0]
    for q in range(1, AZ):
        total = total + a[q] * a[q]
    return total + half_swap(total)


def look_sums(sums, pairs, shift, mine, theirs, powered, lanes):
    swapped = {j: [half_swap(t) for t in theirs[j]] for j in {i + k + 1 - shift for i, k in pairs}}
    for n, (i, k) in enumerate(pairs):
        j = i + k + 1 - shift
        sums[8 * n : 8 * n + 8, lanes] = products(mine[i], theirs[j], swapped[j])
    for m in range(len(powered) // 2):
        one, two = power_of(powered[2 * m]), power_of(powered[2 * m + 1])
        at = 8 * (len(pairs) + m)
        sums[at : at + 8, lanes] = jnp.where(upper(one), one, two)


def fill(sums, tiles_at, halo, body):
    body(halo, pl.ds(0, LANES))
    rows = sums.shape[0]
    sums[:, COLS + LANES :] = sums[:, :LANES].reshape(rows, LANES)

    @pl.loop(0, CHUNKS)
    def _(c):
        body(
            tiles_at(pl.ds(pl.multiple_of(c * LANES, LANES), LANES)),
            pl.ds(pl.multiple_of((c + 1) * LANES, LANES), LANES),
        )


def windows(left):
    k = lax.broadcasted_iota(jnp.int32, (2 * GROUP, GROUP), 0) - LANES
    n = lax.broadcasted_iota(jnp.int32, (2 * GROUP, GROUP), 1)
    band = ((k >= n - MARGIN) & (k < n + MARGIN)).astype(jnp.float32).astype(jnp.bfloat16)
    total = None
    for _ in range(3):
        term = left.astype(jnp.bfloat16)
        left = left - term.astype(jnp.float32)
        part = jnp.dot(term, band, preferred_element_type=jnp.float32)
        total = part if total is None else total + part
    return total


def unpacked_powers(result, base, count):
    powers = []
    for m in range(count // 2):
        both = result[base + 8 * m : base + 8 * m + 8]
        other = half_swap(both)
        powers.append(jnp.where(upper(both), both, other))
        powers.append(jnp.where(upper(both), other, both))
    return powers


def write_pair(store, cross, power_first, power_second, used):
    gamma = cross * (used * lax.rsqrt(jnp.maximum(power_first * power_second, 1.0)))
    square = gamma * gamma
    magnitude = jnp.sqrt(square + half_swap(square))
    store(0, gamma[:LOOKS])
    store(1, gamma[LOOKS:])
    store(2, magnitude[:LOOKS])


def own_tiles(pieces, high, lanes, dates):
    tiles = {}
    for d in dates:
        if d < LAG:
            units = [place(d * AZ + q) for q in range(AZ)]
            tiles[d] = [pieces[n][at, :, lanes] for n, at in units]
        else:
            tiles[d] = [high[d - LAG, q, :, lanes] for q in range(AZ)]
    return tiles


def inner(*refs):
    pieces = refs[:COUNT]
    slc, first, stop, edges, used, out, power, high, sums, buf, sems = refs[COUNT:]
    dates = range(DATES)
    lay_out_last(slc, first, stop, high, buf, sems)

    def body(tiles, lanes):
        powered = [tiles[d] for d in dates]
        look_sums(sums, INNER_PAIRS, 0, tiles, tiles, powered, lanes)

    fill(
        sums,
        lambda lanes: own_tiles(pieces, high, lanes, dates),
        {d: halo_of(edges, d) for d in dates},
        body,
    )
    for g in range(COLS // GROUP):
        lanes = slice(g * GROUP, (g + 1) * GROUP)
        result = windows(sums[:, g * GROUP : (g + 2) * GROUP])
        powers = unpacked_powers(result, 8 * len(INNER_PAIRS), DATES)
        for d in range(OUTER_FIRST, DATES):
            power[d - OUTER_FIRST, :, lanes] = powers[d]
        for n, (i, k) in enumerate(INNER_PAIRS):

            def store(m, value, i=i, k=k, lanes=lanes):
                out[i * LAG + k, m, :, lanes] = value

            write_pair(
                store,
                result[8 * n : 8 * n + 8],
                powers[i],
                powers[i + k + 1],
                used[k, i].astype(jnp.float32),
            )


def write_outer(result, power, used, staged, at, lanes):
    powers = unpacked_powers(result, 8 * len(OUTER_PAIRS), LAG)
    for n, (i, k) in enumerate(OUTER_PAIRS):

        def store(m, value, n=n):
            staged[n, m, :, at : at + GROUP] = value

        write_pair(
            store,
            result[8 * n : 8 * n + 8],
            power[i - OUTER_FIRST, :, lanes],
            powers[i + k + 1 - DATES],
            used[k, i].astype(jnp.float32),
        )


def copies_out(staged, out, sems, parts):
    where = [i * LAG + k for i, k in OUTER_PAIRS]
    heads = [n for n in range(len(where)) if n == 0 or where[n] != where[n - 1] + 1]
    copies = []
    for (at, lane), sem in zip(parts, range(len(parts))):
        width = 2 * GROUP // len(parts)
        for head, following in zip(heads, heads[1:] + [len(where)]):
            size = following - head
            copies.append(
                pltpu.make_async_copy(
                    staged.at[pl.ds(head, size), :, :, pl.ds(at, width)],
                    out.at[pl.ds(where[head], size), :, :, pl.ds(lane, width)],
                    sems.at[sem, heads.index(head)],
                )
            )
    for copy in copies:
        copy.start()
    return copies


def outer_middle(*refs):
    pieces = refs[:COUNT]
    high, power, used, received = refs[COUNT : COUNT + 4]
    far = refs[COUNT + 4 : 2 * COUNT + 4]
    out, sums, staged, sems = refs[2 * COUNT + 5 :]
    dates = range(OUTER_FIRST, DATES)

    @pl.loop(0, CHUNKS)
    def _(c):
        lanes = pl.ds(pl.multiple_of(c * LANES, LANES), LANES)
        theirs = []
        for d in range(LAG):
            units = [d * AZ + q for q in range(AZ)]
            theirs.append(
                [
                    received[unit, :, lanes] + far[place(unit)[0]][place(unit)[1], :, lanes]
                    for unit in units
                ]
            )
        mine = own_tiles(pieces, high, lanes, dates)
        look_sums(sums, OUTER_PAIRS, DATES, mine, theirs, theirs, lanes)

    for g in (1, 2):
        lanes = slice(g * GROUP, (g + 1) * GROUP)
        result = windows(sums[:, g * GROUP - LANES : (g + 2) * GROUP - LANES])
        write_outer(result, power, used, staged, (g - 1) * GROUP, lanes)
    for copy in copies_out(staged, out, sems, [(0, GROUP)]):
        copy.wait()


def outer_sides(sums, edges, power, used, their_edges, out_in, out, halo, staged, sems):
    del out_in
    dates = range(OUTER_FIRST, DATES)
    mine = {d: halo_of(edges, d) for d in dates}
    theirs = [halo_of(their_edges, d) for d in range(LAG)]
    look_sums(halo, OUTER_PAIRS, DATES, mine, theirs, theirs, slice(0, LANES))
    ends = halo[...]
    inside = 2 * GROUP - LANES
    copies = []
    for part, left in enumerate(
        (
            jnp.concatenate([ends, sums[:, :inside]], axis=1),
            jnp.concatenate([sums[:, COLS - inside :], ends], axis=1),
        )
    ):
        lane = part * (COLS - GROUP)
        write_outer(
            windows(left), power, used, staged, part * GROUP, slice(lane, lane + GROUP)
        )
    copies = copies_out(staged, out, sems, [(0, 0), (GROUP, COLS - GROUP)])
    for copy in copies:
        copy.wait()


def far_permutes():
    def flat(x, y, z, core):
        return ((z // 8) * 16 + y * 4 + x) * 16 + (z % 8) * 2 + core

    straight = []
    scatter = [[] for _ in PIECES]
    gather = [[] for _ in PIECES]
    for z in range(8):
        for core in range(2):
            if COLUMN_SETS[z // 2][core] is None:
                straight.append((flat(*SOURCE_XY, 8 + z, core), flat(*TARGET_XY, z, core)))
                continue
            for n, (x, y) in enumerate(COLUMN_SETS[z // 2][core]):
                relay = flat(x, y, 8 + z, core)
                scatter[n].append((flat(*SOURCE_XY, 8 + z, core), relay))
                gather[n].append((relay, flat(*TARGET_XY, z, core)))
    return straight, scatter, gather


def sum_rows(pairs, dates):
    return 8 * (len(pairs) + dates // 2)


def on_device(slc, first_row, stop_row, pair_used):
    slc = slc.reshape(DATES, 2, AZ * LOOKS, CHUNKS, LANES).transpose(0, 2, 3, 1, 4)
    slc = slc.reshape(DATES * PER_DATE, LANES)
    piece_shapes = [f32_vmem(size, 8, COLS) for size in PIECES]
    edge_shape = f32_vmem(2, AZ, 8, LANES)
    *pieces, low, edge_low, edge_high = pl.pallas_call(
        prepare,
        out_shape=piece_shapes + [f32_vmem(LAG * AZ, 8, COLS), edge_shape, edge_shape],
        in_specs=[ANY, SMEM, SMEM],
        out_specs=[VMEM] * (COUNT + 3),
        scratch_shapes=[
            pltpu.VMEM((DATES * PER_DATE, LANES), jnp.float32),
            pltpu.SemaphoreType.DMA((DATES,)),
        ],
        compiler_params=PARAMS,
        name="prepare",
    )(in_hbm(slc), in_hbm(first_row), in_hbm(stop_row))

    def permute(value, pairs):
        return lax.ppermute(value, AXES, pairs)

    near = [
        (d * 16 + c, (d - 1) * 16 + c) for d in range(1, 32) if d != 16 for c in range(16)
    ]
    far = [(16 * 16 + c, 15 * 16 + c) for c in range(16)]
    to_right = [(d * 16 + c, d * 16 + c + 1) for d in range(32) for c in range(15)]
    to_left = [(b, a) for a, b in to_right]
    straight, scatter, gather = far_permutes()

    scattered = [permute(piece, pairs) for piece, pairs in zip(pieces, scatter)]
    left = permute(edge_high, to_right)
    right = permute(edge_low, to_left)
    received = permute(low, near + straight)
    edges = right + left
    gathered = [permute(piece, pairs) for piece, pairs in zip(scattered, gather)]
    their_edges = permute(edges[:1], near + far)

    used = pair_used.T
    out_shape = f32(DATES * LAG, 3, LOOKS, COLS)
    out, power, high = pl.pallas_call(
        inner,
        out_shape=[
            out_shape,
            f32_vmem(DATES - OUTER_FIRST, 8, COLS),
            f32_vmem(DATES - LAG, AZ, 8, COLS),
        ],
        in_specs=[VMEM] * COUNT + [ANY, SMEM, SMEM, VMEM, SMEM],
        out_specs=[VMEM] * 3,
        scratch_shapes=[
            pltpu.VMEM((sum_rows(INNER_PAIRS, DATES), WIDE), jnp.float32),
            pltpu.VMEM(((DATES - LAG) * PER_DATE, LANES), jnp.float32),
            pltpu.SemaphoreType.DMA((DATES - LAG,)),
        ],
        compiler_params=PARAMS,
        name="inner",
    )(*pieces, in_hbm(slc), in_hbm(first_row), in_hbm(stop_row), edges, in_hbm(used))
    rows = sum_rows(OUTER_PAIRS, LAG)
    scratch = pltpu.VMEM((len(OUTER_PAIRS), 3, LOOKS, 2 * GROUP), jnp.float32)
    out, sums = pl.pallas_call(
        outer_middle,
        out_shape=[out_shape, f32_vmem(rows, COLS)],
        in_specs=[VMEM] * (COUNT + 2) + [SMEM] + [VMEM] * (COUNT + 1) + [ANY],
        out_specs=[ANY, VMEM],
        input_output_aliases={2 * COUNT + 4: 0},
        scratch_shapes=[scratch, pltpu.SemaphoreType.DMA((1, 3))],
        compiler_params=PARAMS,
        name="outer_middle",
    )(*pieces, high, power, in_hbm(used), received, *gathered, out)
    out = pl.pallas_call(
        outer_sides,
        out_shape=out_shape,
        in_specs=[VMEM] * 3 + [SMEM, VMEM, ANY],
        out_specs=ANY,
        input_output_aliases={5: 0},
        scratch_shapes=[
            pltpu.VMEM((rows, LANES), jnp.float32),
            scratch,
            pltpu.SemaphoreType.DMA((2, 3)),
        ],
        compiler_params=PARAMS,
        name="outer_sides",
    )(sums, edges, power, in_hbm(used), their_edges, out)
    return out.reshape(DATES, LAG, 3, LOOKS, COLS)


def solution(mesh):
    return jax.shard_map(
        on_device,
        mesh=mesh,
        in_specs=(P("date", None, None, "col"), P("date"), P("date"), P("date", None)),
        out_specs=P("date", None, None, None, "col"),
        check_vma=False,
    )
```
